32 devices in a mesh: dp: 8 (over y, x, core), tensor: 4 (over z).
Axes of the slice: x: 2, y: 2, z: 4, core: 2. Of those that a mesh axis runs over, the one named last changes fastest.
Arguments:
- out_grad: bfloat16 [16384, 512], P('dp'), may hold values from -0.0625 to 0.0625
- inputs: bfloat16 [16384, 8192], P('dp', 'tensor'), may hold values from -6 to 6
- weights: float32 [512, 8192], P('dp', 'tensor'), may hold values from -60 to 60
- moment: float32 [512, 8192], P('dp', 'tensor'), may hold values from -3 to 3
- second: float32 [512, 8192], P('dp', 'tensor'), may hold values from 0.05 to 2
Outputs:
- new_weights: float32 [512, 8192], P('dp', 'tensor')
- new_moment: float32 [512, 8192], P('dp', 'tensor')
- new_second: float32 [512, 8192], P('dp', 'tensor')
The draws below stay inside these ranges and needn't reach their ends.
All inputs are finite; a program needn't handle non-finite values.
Results may differ from the reference program's by a relative error of at most 0.0003.
Values sent between devices are 32-bit elements; how exact they have to be, the bound alone decides.
A program may use at most 128 MiB of HBM per device.

```python
import math
import jax
import jax.numpy as jnp
from jax import lax

D = 8192
ROWS = 512
TOKENS = 16384


def draw_weights(key, part):
    key = jax.random.fold_in(key, 7)
    first, col_key, row_key = jax.random.split(key, 3)
    ramp = 3.0 ** (jnp.arange(D, dtype=jnp.float32) / D)
    col_scale = 10.0 ** jax.random.uniform(col_key, (1, D), jnp.float32)
    row_scale = 10.0 ** jax.random.uniform(row_key, (ROWS, 1), jnp.float32)
    base = jnp.clip(jax.random.normal(first, (ROWS, D), jnp.float32), -6.0, 6.0)
    return 0.03 * base * ramp[None, :] * col_scale * row_scale


def spiked(array, own_key, source, target, parts, factor):
    owner, partner = [(jnp.arange(array.shape[dim]) // (array.shape[dim] // parts)).reshape([-1 if axis == dim else 1 for axis in range(array.ndim)]) for dim in (source, target)]
    chosen = jax.random.permutation(own_key, parts)[partner]
    strong = (owner == chosen) | (owner == (partner + parts // 2) % parts)
    return jnp.where(strong, factor * array, array)


def block_scale(key, dims, pieces, least, largest):
    level, own = 1.0, jax.random.fold_in(key, 6)
    for position, parts in pieces:
        draws = jnp.exp(jax.random.uniform(jax.random.fold_in(own, position), (parts,), jnp.float32, least / len(pieces), largest / len(pieces)))
        level = level * jnp.repeat(draws, dims[position] // parts).reshape([-1 if axis == position else 1 for axis in range(len(dims))])
    return level


def scatter_about(stream_key, dims, spread, reach, cuts=(), kind=jnp.bfloat16):
    entries = spread * jax.random.normal(stream_key, dims, jnp.float32)
    if cuts:
        entries = entries * block_scale(stream_key, dims, cuts, -0.22, 0.18)
    return jnp.clip(entries, -reach, reach).astype(kind)


def gaussian_with(own_key, shape, deviation, reach, cuts, heavy, kind=jnp.bfloat16):
    values = deviation * jax.random.normal(own_key, shape, jnp.float32)
    if cuts:
        values = values * block_scale(own_key, shape, cuts, -0.22, 0.18)
    return jnp.clip(spiked(values, jax.random.fold_in(own_key, 3), *heavy), -reach, reach).astype(kind)


def setup_inputs(seed: int = 0) -> dict:
    streams_of = jax.random.split(jax.random.key(seed), 6)
    return {
        "out_grad": gaussian_with(streams_of[0], (TOKENS, ROWS), TOKENS ** -0.5, 0.0625, ((0, 8),), (0, 1, 8, 2.0)),
        "inputs": scatter_about(streams_of[1], (TOKENS, D), 1.0, 6.0, ((0, 8), (1, 4))),
        "weights": draw_weights(jax.random.fold_in(streams_of[5], 71), 0),
        "moment": scatter_about(streams_of[3], (ROWS, D), 0.3, 3.0, ((0, 8), (1, 4)), jnp.float32),
        "second": jnp.clip(jnp.exp(math.log(2.0) - 3.6888794 * jax.random.uniform(streams_of[4], (ROWS, D), jnp.float32) ** block_scale(streams_of[4], (ROWS, D), ((0, 8), (1, 4)), -0.2, 0.2)), 0.05, 2.0),
    }


def finish(grad, weights, moment, second):
    new_moment = 0.9 * moment + 0.1 * grad
    new_second = 0.95 * second + 0.05 * grad * grad
    step_size = 0.3 * (new_moment / (1.0 - 0.9 ** 10))
    moved = weights - step_size / (jnp.sqrt(new_second / (1.0 - 0.95 ** 10)) + 1e-08)
    return (moved, new_moment, new_second)

def reference(out_grad, inputs, weights, moment, second):
    grad = lax.dot_general(out_grad, inputs, (((0,), (0,)), ((), ())), preferred_element_type=jnp.float32)
    moved, new_moment, new_second = finish(grad, weights, moment, second)
    mean_square = lax.optimization_barrier(jnp.mean(moved * moved, axis=1, keepdims=True))
    new_weights = moved / jnp.sqrt(mean_square + 1e-06)
    return (new_weights, new_moment, new_second)
```

```python
import functools

import jax
import jax.numpy as jnp
from jax import lax
from jax.experimental import pallas as pl
from jax.experimental.pallas import tpu as pltpu
from jax.sharding import PartitionSpec as P

MESH = pl.DeviceIdType.MESH
CHUNK = 256
SLOTS = 4
GROUP = 512
LAG = 3


def finish(grad, weights, moment, second):
    new_moment = 0.9 * moment + 0.1 * grad
    new_second = 0.95 * second + 0.05 * grad * grad
    step_size = 0.3 * (new_moment / (1.0 - 0.9**10))
    moved = weights - step_size / (jnp.sqrt(new_second / (1.0 - 0.95**10)) + 1e-08)
    return (moved, new_moment, new_second)


def bit(index, b):
    return lax.rem(index // (1 << b), 2)


def kernel(
    dp, nt, og_hbm, in_hbm, w_hbm, m_hbm, s_hbm, out_w, out_m, out_s, *scratch
):
    bits = dp.bit_length() - 1
    og, og_t, ins, wms, res, acc, tot, zsend, zrecv = scratch[:9]
    recv = scratch[9 : 9 + bits]
    og_sem, in_sem, wms_sem, out_sem, send_sem, recv_sem, zs_sem, zr_sem = scratch[9 + bits :]
    tokens, rows = og.shape
    block = rows // dp
    width = w_hbm.shape[1]
    n = width // CHUNK
    me, z = lax.axis_index("dp"), lax.axis_index("tensor")

    plane = (bits - 1) // 2
    along_x = list(range(1, 1 + plane))
    along_y = list(range(1 + plane, bits))
    orders = ([0] + along_x + along_y, [0] + along_y + along_x)

    def partner(b):
        mine = bit(me, b)
        return (me + (1 - 2 * mine) * (1 << b), z)

    def cols(j):
        return slice(j * CHUNK, (j + 1) * CHUNK)

    def in_copy(j):
        return pltpu.make_async_copy(
            in_hbm.at[:, cols(j)], ins.at[j % SLOTS], in_sem.at[j % SLOTS]
        )

    def exchange(s, j):
        half = dp >> (s + 1)
        return pltpu.make_async_remote_copy(
            src_ref=acc.at[j, pl.ds(half, half)],
            dst_ref=recv[s].at[j],
            send_sem=send_sem.at[s, j],
            recv_sem=recv_sem.at[s, j],
            device_id=partner(orders[j % 2][s]),
            device_id_type=MESH,
        )

    og_copy = pltpu.make_async_copy(og_hbm, og, og_sem)
    og_copy.start()
    for j in range(min(SLOTS, n)):
        in_copy(j).start()
    wms_copies = [
        pltpu.make_async_copy(ref, wms.at[i], wms_sem.at[i])
        for i, ref in enumerate((w_hbm, m_hbm, s_hbm))
    ]
    for copy in wms_copies:
        copy.start()

    barrier = pltpu.get_barrier_semaphore()
    peers = [lax.rem(z + d, nt) for d in range(1, nt)]
    for b in range(bits):
        pl.semaphore_signal(barrier, inc=1, device_id=partner(b), device_id_type=MESH)
    for peer in peers:
        pl.semaphore_signal(barrier, inc=1, device_id=(me, peer), device_id_type=MESH)

    tile = 256
    eye = (
        lax.broadcasted_iota(jnp.int32, (tile, tile), 0)
        == lax.broadcasted_iota(jnp.int32, (tile, tile), 1)
    ).astype(jnp.bfloat16)
    og_copy.wait()

    @pl.loop(0, rows // tile)
    def _(r):
        at = pl.ds(pl.multiple_of(r * tile, tile), tile)
        for k in range(tokens // tile):
            ks = slice(k * tile, (k + 1) * tile)
            og_t[at, ks] = lax.dot_general(
                eye, og[ks, at], (((1,), (1,)), ((), ())), preferred_element_type=jnp.float32
            ).astype(jnp.bfloat16)

    def multiply(j):
        in_copy(j).wait()

        def group(g, _):
            at = pl.ds(pl.multiple_of(g * GROUP, GROUP), GROUP)
            part = jnp.dot(
                og_t[at, :], ins[j % SLOTS], preferred_element_type=jnp.float32
            )
            for o in range(GROUP // block):
                owner = g * (GROUP // block) + o
                place = 0
                for s, b in enumerate(orders[j % 2]):
                    place += lax.rem(bit(me, b) + bit(owner, b), 2) * (dp >> (s + 1))
                acc[j, place] = part[o * block : (o + 1) * block]
            return 0

        lax.fori_loop(0, rows // GROUP, group, 0)
        if j + SLOTS < n:
            in_copy(j + SLOTS).start()

    def out_copies(j):
        return [
            pltpu.make_async_copy(
                res.at[i, :, cols(j)], ref.at[:, cols(j)], out_sem.at[i, j]
            )
            for i, ref in enumerate((out_w, out_m, out_s))
        ]

    def receive(s, j):
        half = dp >> (s + 1)
        exchange(s, j).wait_recv()
        if s < bits - 1:
            acc[j, pl.ds(0, half)] += recv[s][j]
            exchange(s + 1, j).start()
            return
        if j == 0:
            for copy in wms_copies:
                copy.wait()
        grad = acc[j, 0] + recv[s][j, 0]
        moved, new_moment, new_second = finish(
            grad, wms[0, :, cols(j)], wms[1, :, cols(j)], wms[2, :, cols(j)]
        )
        res[0, :, cols(j)] = moved
        res[1, :, cols(j)] = new_moment
        res[2, :, cols(j)] = new_second
        for copy in out_copies(j)[1:]:
            copy.start()
        square = moved * moved
        part = square[:, :128]
        for c in range(1, CHUNK // 128):
            part += square[:, c * 128 : (c + 1) * 128]
        tot[...] = part if j == 0 else tot[...] + part

    for j in range(n):
        multiply(j)
        if j == 0:
            pl.semaphore_wait(barrier, bits + nt - 1)
        exchange(0, j).start()
        if j >= 1:
            receive(0, j - 1)
    receive(0, n - 1)
    for i in range(n + LAG * (bits - 2)):
        for s in range(1, bits):
            j = i - LAG * (s - 1)
            if 0 <= j < n:
                receive(s, j)

    exact = lax.Precision.HIGHEST
    zsend[...] = lax.dot_general(
        jnp.ones((8, 128), jnp.float32),
        tot[...],
        (((1,), (1,)), ((), ())),
        precision=exact,
        preferred_element_type=jnp.float32,
    )

    def share(d):
        return pltpu.make_async_remote_copy(
            src_ref=zsend,
            dst_ref=zrecv.at[d],
            send_sem=zs_sem.at[d],
            recv_sem=zr_sem.at[d],
            device_id=(me, peers[d]),
            device_id_type=MESH,
        )

    for d in range(nt - 1):
        share(d).start()
    total = zsend[...]
    for d in range(nt - 1):
        share(d).wait_recv()
        total = total + zrecv[d]
    row_total = lax.dot_general(
        total,
        jnp.full((8, 128), 0.125, jnp.float32),
        (((0,), (0,)), ((), ())),
        precision=exact,
        preferred_element_type=jnp.float32,
    )
    scale = lax.rsqrt(row_total / (width * nt) + 1e-06)
    for c in range(width // 128):
        cs = slice(c * 128, (c + 1) * 128)
        res[0, :, cs] = res[0, :, cs] * scale
        if (c + 1) * 128 % CHUNK == 0:
            out_copies(c * 128 // CHUNK)[0].start()
    for d in range(nt - 1):
        share(d).wait_send()
    for s in range(bits):
        for j in range(n):
            exchange(s, j).wait_send()
    for j in range(n):
        for copy in out_copies(j):
            copy.wait()


def on_device(dp, nt, out_grad, inputs, weights, moment, second):
    tokens, rows = out_grad.shape
    block, width = weights.shape
    n = width // CHUNK
    bits = dp.bit_length() - 1
    dma = pltpu.SemaphoreType.DMA
    scratch = [
        pltpu.VMEM((tokens, rows), jnp.bfloat16),
        pltpu.VMEM((rows, tokens), jnp.bfloat16),
        pltpu.VMEM((SLOTS, tokens, CHUNK), jnp.bfloat16),
        pltpu.VMEM((3, block, width), jnp.float32),
        pltpu.VMEM((3, block, width), jnp.float32),
        pltpu.VMEM((n, dp, block, CHUNK), jnp.float32),
        pltpu.VMEM((block, 128), jnp.float32),
        pltpu.VMEM((8, block), jnp.float32),
        pltpu.VMEM((nt - 1, 8, block), jnp.float32),
    ]
    scratch += [
        pltpu.VMEM((n, dp >> (s + 1), block, CHUNK), jnp.float32) for s in range(bits)
    ]
    scratch += [
        dma,
        dma((SLOTS,)),
        dma((3,)),
        dma((3, n)),
        dma((bits, n)),
        dma((bits, n)),
        dma((nt - 1,)),
        dma((nt - 1,)),
    ]
    return pl.pallas_call(
        functools.partial(kernel, dp, nt),
        out_shape=[jax.ShapeDtypeStruct(weights.shape, jnp.float32)] * 3,
        in_specs=[pl.BlockSpec(memory_space=pl.ANY)] * 5,
        out_specs=[pl.BlockSpec(memory_space=pl.ANY)] * 3,
        scratch_shapes=scratch,
        compiler_params=pltpu.CompilerParams(
            collective_id=0, has_side_effects=True, vmem_limit_bytes=60 << 20
        ),
    )(out_grad, inputs, weights, moment, second)


def solution(mesh):
    held = P("dp", "tensor")
    return jax.shard_map(
        functools.partial(on_device, mesh.shape["dp"], mesh.shape["tensor"]),
        mesh=mesh,
        in_specs=(P("dp", None), held, held, held, held),
        out_specs=(held, held, held),
        check_vma=False,
    )
```

```python
import functools
import math

import jax
import jax.numpy as jnp
from jax import lax
from jax.experimental import pallas as pl
from jax.experimental.pallas import tpu as pltpu
from jax.sharding import PartitionSpec as P

MESH = pl.DeviceIdType.MESH
CHUNK = 256
SLOTS = 4
GROUP = 512
LAG = 3


def finish(grad, weights, moment, second):
    new_moment = 0.9 * moment + 0.1 * grad
    new_second = 0.95 * second + 0.05 * grad * grad
    step_size = 0.3 * (new_moment / (1.0 - 0.9**10))
    moved = weights - step_size / (jnp.sqrt(new_second / (1.0 - 0.95**10)) + 1e-08)
    return (moved, new_moment, new_second)


def bit(index, b):
    return lax.rem(index // (1 << b), 2)


def kernel(
    dp, nt, og_hbm, in_hbm, w_hbm, m_hbm, s_hbm, out_w, out_m, out_s, *scratch
):
    bits = dp.bit_length() - 1
    og, og_t, ins, wms, acc, tot, zsend, zrecv = scratch[:8]
    recv = scratch[8 : 8 + bits]
    og_sem, in_sem, wms_sem, send_sem, recv_sem, zs_sem, zr_sem = scratch[8 + bits :]
    tokens, rows = og.shape
    block = rows // dp
    width = w_hbm.shape[1]
    n = width // CHUNK
    me, z = lax.axis_index("dp"), lax.axis_index("tensor")

    plane = (bits - 1) // 2
    along_x = list(range(1, 1 + plane))
    along_y = list(range(1 + plane, bits))
    orders = ([0] + along_x + along_y, [0] + along_y + along_x)

    def partner(b):
        mine = bit(me, b)
        return (me + (1 - 2 * mine) * (1 << b), z)

    def cols(j):
        return slice(j * CHUNK, (j + 1) * CHUNK)

    def in_copy(j):
        return pltpu.make_async_copy(
            in_hbm.at[:, cols(j)], ins.at[j % SLOTS], in_sem.at[j % SLOTS]
        )

    def exchange(s, j):
        half = dp >> (s + 1)
        return pltpu.make_async_remote_copy(
            src_ref=acc.at[j, pl.ds(half, half)],
            dst_ref=recv[s].at[j],
            send_sem=send_sem.at[s, j],
            recv_sem=recv_sem.at[s, j],
            device_id=partner(orders[j % 2][s]),
            device_id_type=MESH,
        )

    og_copy = pltpu.make_async_copy(og_hbm, og, og_sem)
    og_copy.start()
    for j in range(min(SLOTS, n)):
        in_copy(j).start()
    wms_copies = [
        pltpu.make_async_copy(ref, wms.at[i], wms_sem.at[i])
        for i, ref in enumerate((w_hbm, m_hbm, s_hbm))
    ]
    for copy in wms_copies:
        copy.start()

    barrier = pltpu.get_barrier_semaphore()
    peers = [lax.rem(z + d, nt) for d in range(1, nt)]
    for b in range(bits):
        pl.semaphore_signal(barrier, inc=1, device_id=partner(b), device_id_type=MESH)
    for peer in peers:
        pl.semaphore_signal(barrier, inc=1, device_id=(me, peer), device_id_type=MESH)

    tile = 256
    eye = (
        lax.broadcasted_iota(jnp.int32, (tile, tile), 0)
        == lax.broadcasted_iota(jnp.int32, (tile, tile), 1)
    ).astype(jnp.bfloat16)
    og_copy.wait()

    @pl.loop(0, rows // tile)
    def _(r):
        at = pl.ds(pl.multiple_of(r * tile, tile), tile)
        for k in range(tokens // tile):
            ks = slice(k * tile, (k + 1) * tile)
            og_t[at, ks] = lax.dot_general(
                eye, og[ks, at], (((1,), (1,)), ((), ())), preferred_element_type=jnp.float32
            ).astype(jnp.bfloat16)

    def multiply(j):
        in_copy(j).wait()

        def group(g, _):
            at = pl.ds(pl.multiple_of(g * GROUP, GROUP), GROUP)
            part = jnp.dot(
                og_t[at, :], ins[j % SLOTS], preferred_element_type=jnp.float32
            )
            for o in range(GROUP // block):
                owner = g * (GROUP // block) + o
                place = 0
                for s, b in enumerate(orders[j % 2]):
                    place += lax.rem(bit(me, b) + bit(owner, b), 2) * (dp >> (s + 1))
                acc[j, place] = part[o * block : (o + 1) * block]
            return 0

        lax.fori_loop(0, rows // GROUP, group, 0)
        if j + SLOTS < n:
            in_copy(j + SLOTS).start()

    def receive(s, j):
        half = dp >> (s + 1)
        exchange(s, j).wait_recv()
        if s < bits - 1:
            acc[j, pl.ds(0, half)] += recv[s][j]
            exchange(s + 1, j).start()
            return
        if j == 0:
            for copy in wms_copies:
                copy.wait()
        grad = acc[j, 0] + recv[s][j, 0]
        moved, new_moment, new_second = finish(
            grad, wms[0, :, cols(j)], wms[1, :, cols(j)], wms[2, :, cols(j)]
        )
        out_w[:, cols(j)] = moved
        out_m[:, cols(j)] = new_moment
        out_s[:, cols(j)] = new_second
        square = moved * moved
        part = square[:, :128]
        for c in range(1, CHUNK // 128):
            part += square[:, c * 128 : (c + 1) * 128]
        tot[...] = part if j == 0 else tot[...] + part

    for j in range(n):
        multiply(j)
        if j == 0:
            pl.semaphore_wait(barrier, bits + nt - 1)
        exchange(0, j).start()
        if j >= 1:
            receive(0, j - 1)
    receive(0, n - 1)
    for i in range(n + LAG * (bits - 2)):
        for s in range(1, bits):
            j = i - LAG * (s - 1)
            if 0 <= j < n:
                receive(s, j)

    exact = lax.Precision.HIGHEST
    zsend[...] = lax.dot_general(
        jnp.ones((8, 128), jnp.float32),
        tot[...],
        (((1,), (1,)), ((), ())),
        precision=exact,
        preferred_element_type=jnp.float32,
    )

    def share(d):
        return pltpu.make_async_remote_copy(
            src_ref=zsend,
            dst_ref=zrecv.at[d],
            send_sem=zs_sem.at[d],
            recv_sem=zr_sem.at[d],
            device_id=(me, peers[d]),
            device_id_type=MESH,
        )

    for d in range(nt - 1):
        share(d).start()
    total = zsend[...]
    for d in range(nt - 1):
        share(d).wait_recv()
        total = total + zrecv[d]
    row_total = lax.dot_general(
        total,
        jnp.full((8, 128), 0.125, jnp.float32),
        (((0,), (0,)), ((), ())),
        precision=exact,
        preferred_element_type=jnp.float32,
    )
    scale = lax.rsqrt(row_total / (width * nt) + 1e-06)
    for c in range(width // 128):
        cs = slice(c * 128, (c + 1) * 128)
        out_w[:, cs] = out_w[:, cs] * scale
    for d in range(nt - 1):
        share(d).wait_send()
    for s in range(bits):
        for j in range(n):
            exchange(s, j).wait_send()


def on_device(dp, nt, out_grad, inputs, weights, moment, second):
    tokens, rows = out_grad.shape
    block, width = weights.shape
    n = width // CHUNK
    bits = dp.bit_length() - 1
    dma = pltpu.SemaphoreType.DMA
    scratch = [
        pltpu.VMEM((tokens, rows), jnp.bfloat16),
        pltpu.VMEM((rows, tokens), jnp.bfloat16),
        pltpu.VMEM((SLOTS, tokens, CHUNK), jnp.bfloat16),
        pltpu.VMEM((3, block, width), jnp.float32),
        pltpu.VMEM((n, dp, block, CHUNK), jnp.float32),
        pltpu.VMEM((block, 128), jnp.float32),
        pltpu.VMEM((8, block), jnp.float32),
        pltpu.VMEM((nt - 1, 8, block), jnp.float32),
    ]
    scratch += [
        pltpu.VMEM((n, dp >> (s + 1), block, CHUNK), jnp.float32) for s in range(bits)
    ]
    scratch += [
        dma,
        dma((SLOTS,)),
        dma((3,)),
        dma((bits, n)),
        dma((bits, n)),
        dma((nt - 1,)),
        dma((nt - 1,)),
    ]
    held = sum(
        jnp.dtype(ref.dtype).itemsize * math.prod(ref.shape)
        for ref in scratch
        if getattr(ref, "memory_space", None) == pltpu.VMEM
    )
    return pl.pallas_call(
        functools.partial(kernel, dp, nt),
        out_shape=[pltpu.VMEM(weights.shape, jnp.float32)] * 3,
        in_specs=[pl.BlockSpec(memory_space=pltpu.HBM)] * 5,
        out_specs=[pl.BlockSpec(memory_space=pltpu.VMEM)] * 3,
        scratch_shapes=scratch,
        compiler_params=pltpu.CompilerParams(
            collective_id=0, has_side_effects=True, vmem_limit_bytes=held + (3 << 20)
        ),
    )(
        *(
            pltpu.with_memory_space_constraint(x, pltpu.HBM)
            for x in (out_grad, inputs, weights, moment, second)
        )
    )


def solution(mesh):
    held = P("dp", "tensor")
    return jax.shard_map(
        functools.partial(on_device, mesh.shape["dp"], mesh.shape["tensor"]),
        mesh=mesh,
        in_specs=(P("dp", None), held, held, held, held),
        out_specs=(held, held, held),
        check_vma=False,
    )
```

```python
import functools
import math

import jax
import jax.numpy as jnp
from jax import lax
from jax.experimental import pallas as pl
from jax.experimental.pallas import tpu as pltpu
from jax.sharding import PartitionSpec as P

MESH = pl.DeviceIdType.MESH
CHUNK = 256
SLOTS = 4
GROUP = 512
LAG = 3
PIECES = 4
SPLIT = 2


def finish(grad, weights, moment, second):
    new_moment = 0.9 * moment + 0.1 * grad
    new_second = 0.95 * second + 0.05 * grad * grad
    step_size = 0.3 * (new_moment / (1.0 - 0.9**10))
    moved = weights - step_size / (jnp.sqrt(new_second / (1.0 - 0.95**10)) + 1e-08)
    return (moved, new_moment, new_second)


def bit(index, b):
    return lax.rem(index // (1 << b), 2)


def kernel(
    dp, nt, og_hbm, in_hbm, w_hbm, m_hbm, s_hbm, moved_ref, moment_ref, second_ref, out_scale, *scratch
):
    bits = dp.bit_length() - 1
    og, og_t, ins, wms, acc, tot, zsend, zrecv = scratch[:8]
    recv = scratch[8 : 8 + bits]
    og_sem, in_sem, wms_sem, send_sem, recv_sem, zs_sem, zr_sem = scratch[8 + bits :]
    tokens, rows = og.shape
    block = rows // dp
    width = w_hbm.shape[1]
    n = width // CHUNK
    me, z = lax.axis_index("dp"), lax.axis_index("tensor")

    plane = (bits - 1) // 2
    along_x = list(range(1, 1 + plane))
    along_y = list(range(1 + plane, bits))
    orders = ([0] + along_x + along_y, [0] + along_y + along_x)

    def partner(b):
        mine = bit(me, b)
        return (me + (1 - 2 * mine) * (1 << b), z)

    def cols(j):
        return slice(j * CHUNK, (j + 1) * CHUNK)

    def in_copy(j):
        return pltpu.make_async_copy(
            in_hbm.at[:, cols(j)], ins.at[j % SLOTS], in_sem.at[j % SLOTS]
        )

    def exchange(s, j):
        half = dp >> (s + 1)
        return pltpu.make_async_remote_copy(
            src_ref=acc.at[j, pl.ds(half, half)],
            dst_ref=recv[s].at[j],
            send_sem=send_sem.at[s, j],
            recv_sem=recv_sem.at[s, j],
            device_id=partner(orders[j % 2][s]),
            device_id_type=MESH,
        )

    piece = tokens // PIECES

    def og_copy(p):
        at = slice(p * piece, (p + 1) * piece)
        return pltpu.make_async_copy(og_hbm.at[at], og.at[at], og_sem.at[p])

    for p in range(PIECES):
        og_copy(p).start()
    in_copy(0).start()
    wms_copies = [
        pltpu.make_async_copy(ref, wms.at[i], wms_sem.at[i])
        for i, ref in enumerate((w_hbm, m_hbm, s_hbm))
    ]

    barrier = pltpu.get_barrier_semaphore()
    peers = [lax.rem(z + d, nt) for d in range(1, nt)]
    for b in range(bits):
        pl.semaphore_signal(barrier, inc=1, device_id=partner(b), device_id_type=MESH)
    for peer in peers:
        pl.semaphore_signal(barrier, inc=1, device_id=(me, peer), device_id_type=MESH)

    tile = 256
    place_of = lax.broadcasted_iota(jnp.int32, (tile, tile), 0)
    row_of = lax.broadcasted_iota(jnp.int32, (tile, tile), 1)
    own = place_of // (tile // 2)
    pair = (place_of % (tile // 2)) // block
    core = bit(me, 0)
    wanted = (2 * pair + 1 - core + own * (2 * core - 1)) * block + place_of % block
    select = (wanted == row_of).astype(jnp.bfloat16)
    for p in range(PIECES):
        og_copy(p).wait()
        if p == PIECES - 1:
            for j in range(1, min(SLOTS, n)):
                in_copy(j).start()

        def transpose(r, _, p=p):
            rs = pl.ds(pl.multiple_of(r * tile, tile), tile)
            for k in range(p * piece // tile, (p + 1) * piece // tile):
                ks = slice(k * tile, (k + 1) * tile)
                turned = lax.dot_general(
                    select,
                    og[ks, rs],
                    (((1,), (1,)), ((), ())),
                    preferred_element_type=jnp.float32,
                ).astype(jnp.bfloat16)
                for h in range(2):
                    at = h * (rows // 2) + r * (tile // 2)
                    og_t[pl.ds(pl.multiple_of(at, tile // 2), tile // 2), ks] = turned[
                        h * (tile // 2) : (h + 1) * (tile // 2)
                    ]
            return 0

        lax.fori_loop(0, rows // tile, transpose, 0, unroll=rows <= 2 * tile)

    def multiply(j, size, first, last):
        def group(g, _):
            at = pl.ds(pl.multiple_of(g * size, size), size)
            part = jnp.dot(
                og_t[at, :], ins[j % SLOTS], preferred_element_type=jnp.float32
            )
            for o in range(size // block):
                at = g * (size // block) + o
                place = (1 - at // (dp // 2)) * (dp // 2)
                for s, b in enumerate(orders[j % 2]):
                    if s:
                        place += lax.rem(bit(me, b) + bit(at, b - 1), 2) * (dp >> (s + 1))
                acc[j, place] = part[o * block : (o + 1) * block]
            return 0

        lax.fori_loop(first // size, last // size, group, 0)

    def receive(s, j):
        half = dp >> (s + 1)
        exchange(s, j).wait_recv()
        if s < bits - 1:
            acc[j, pl.ds(0, half)] += recv[s][j]
            exchange(s + 1, j).start()
            return
        if j == 0:
            for copy in wms_copies:
                copy.wait()
        grad = acc[j, 0] + recv[s][j, 0]
        moved, new_moment, new_second = finish(
            grad, wms[0, :, cols(j)], wms[1, :, cols(j)], wms[2, :, cols(j)]
        )
        moved_ref[:, cols(j)] = moved
        moment_ref[:, cols(j)] = new_moment
        second_ref[:, cols(j)] = new_second
        square = moved * moved
        part = square[:, :128]
        for c in range(1, CHUNK // 128):
            part += square[:, c * 128 : (c + 1) * 128]
        tot[...] = part if j == 0 else tot[...] + part

    for j in range(n):
        in_copy(j).wait()
        if j < SPLIT:
            multiply(j, GROUP // 2, 0, rows // 2)
            if j == 0:
                pl.semaphore_wait(barrier, bits + nt - 1)
            exchange(0, j).start()
            multiply(j, GROUP // 2, rows // 2, rows)
        else:
            multiply(j, GROUP, 0, rows)
            exchange(0, j).start()
        if j == 0:
            for copy in wms_copies:
                copy.start()
        if j + SLOTS < n:
            in_copy(j + SLOTS).start()
        if j >= 1:
            receive(0, j - 1)
    receive(0, n - 1)
    for i in range(n + LAG * (bits - 2)):
        for s in range(1, bits):
            j = i - LAG * (s - 1)
            if 0 <= j < n:
                receive(s, j)

    exact = lax.Precision.HIGHEST
    zsend[...] = lax.dot_general(
        jnp.ones((8, 128), jnp.float32),
        tot[...],
        (((1,), (1,)), ((), ())),
        precision=exact,
        preferred_element_type=jnp.float32,
    )

    def share(d):
        return pltpu.make_async_remote_copy(
            src_ref=zsend,
            dst_ref=zrecv.at[d],
            send_sem=zs_sem.at[d],
            recv_sem=zr_sem.at[d],
            device_id=(me, peers[d]),
            device_id_type=MESH,
        )

    for d in range(nt - 1):
        share(d).start()
    total = zsend[...]
    for d in range(nt - 1):
        share(d).wait_recv()
        total = total + zrecv[d]
    row_total = lax.dot_general(
        total,
        jnp.full((8, 128), 0.125, jnp.float32),
        (((0,), (0,)), ((), ())),
        precision=exact,
        preferred_element_type=jnp.float32,
    )
    out_scale[...] = lax.rsqrt(row_total / (width * nt) + 1e-06)
    for d in range(nt - 1):
        share(d).wait_send()
    for s in range(bits):
        for j in range(n):
            exchange(s, j).wait_send()


def write_kernel(moved, moment, second, scale, out_w, out_m, out_s, scaled, sem):
    copies = [
        pltpu.make_async_copy(src, dst, sem.at[i])
        for i, (src, dst) in enumerate(((scaled, out_w), (moment, out_m), (second, out_s)))
    ]
    copies[1].start()
    copies[2].start()
    for c in range(moved.shape[1] // 128):
        cs = slice(c * 128, (c + 1) * 128)
        scaled[:, cs] = moved[:, cs] * scale[...]
    copies[0].start()
    for copy in copies:
        copy.wait()


def on_device(dp, nt, out_grad, inputs, weights, moment, second):
    tokens, rows = out_grad.shape
    block, width = weights.shape
    n = width // CHUNK
    bits = dp.bit_length() - 1
    dma = pltpu.SemaphoreType.DMA
    scratch = [
        pltpu.VMEM((tokens, rows), jnp.bfloat16),
        pltpu.VMEM((rows, tokens), jnp.bfloat16),
        pltpu.VMEM((SLOTS, tokens, CHUNK), jnp.bfloat16),
        pltpu.VMEM((3, block, width), jnp.float32),
        pltpu.VMEM((n, dp, block, CHUNK), jnp.float32),
        pltpu.VMEM((block, 128), jnp.float32),
        pltpu.VMEM((8, block), jnp.float32),
        pltpu.VMEM((nt - 1, 8, block), jnp.float32),
    ]
    scratch += [
        pltpu.VMEM((n, dp >> (s + 1), block, CHUNK), jnp.float32) for s in range(bits)
    ]
    scratch += [
        dma((PIECES,)),
        dma((SLOTS,)),
        dma((3,)),
        dma((bits, n)),
        dma((bits, n)),
        dma((nt - 1,)),
        dma((nt - 1,)),
    ]
    held = sum(
        jnp.dtype(ref.dtype).itemsize * math.prod(ref.shape)
        for ref in scratch
        if getattr(ref, "memory_space", None) == pltpu.VMEM
    )
    shapes = [weights.shape] * 3 + [(block, 128)]
    results = pl.pallas_call(
        functools.partial(kernel, dp, nt),
        out_shape=[pltpu.VMEM(shape, jnp.float32) for shape in shapes],
        in_specs=[pl.BlockSpec(memory_space=pltpu.HBM)] * 5,
        out_specs=[pl.BlockSpec(memory_space=pltpu.VMEM)] * 4,
        scratch_shapes=scratch,
        compiler_params=pltpu.CompilerParams(
            collective_id=0, has_side_effects=True, vmem_limit_bytes=held + (3 << 20)
        ),
    )(
        *(
            pltpu.with_memory_space_constraint(x, pltpu.HBM)
            for x in (out_grad, inputs, weights, moment, second)
        )
    )
    return pl.pallas_call(
        write_kernel,
        out_shape=[pltpu.HBM(weights.shape, jnp.float32)] * 3,
        in_specs=[pl.BlockSpec(memory_space=pltpu.VMEM)] * 4,
        out_specs=[pl.BlockSpec(memory_space=pltpu.HBM)] * 3,
        scratch_shapes=[pltpu.VMEM(weights.shape, jnp.float32), dma((3,))],
        compiler_params=pltpu.CompilerParams(vmem_limit_bytes=2 << 20),
    )(*results)


def solution(mesh):
    held = P("dp", "tensor")
    return jax.shard_map(
        functools.partial(on_device, mesh.shape["dp"], mesh.shape["tensor"]),
        mesh=mesh,
        in_specs=(P("dp", None), held, held, held, held),
        out_specs=(held, held, held),
        check_vma=False,
    )
```

```python
import functools
import math

import jax
import jax.numpy as jnp
from jax import lax
from jax.experimental import pallas as pl
from jax.experimental.pallas import tpu as pltpu
from jax.sharding import PartitionSpec as P

MESH = pl.DeviceIdType.MESH
CHUNK = 256
PART = 128
SLOTS = 4
GROUP = 512
LAG = 6
PIECES = 4
SPLIT = 2


def finish(grad, weights, moment, second):
    new_moment = 0.9 * moment + 0.1 * grad
    new_second = 0.95 * second + 0.05 * grad * grad
    step_size = 0.3 * (new_moment / (1.0 - 0.9**10))
    moved = weights - step_size / (jnp.sqrt(new_second / (1.0 - 0.95**10)) + 1e-08)
    return (moved, new_moment, new_second)


def bit(index, b):
    return lax.rem(index // (1 << b), 2)


def kernel(
    dp, nt, og_hbm, in_hbm, w_hbm, m_hbm, s_hbm, moved_ref, moment_ref, second_ref, out_scale, *scratch
):
    bits = dp.bit_length() - 1
    og, og_t, ins, wms, acc, tot, zsend, zrecv = scratch[:8]
    recv = scratch[8 : 8 + bits]
    og_sem, in_sem, wms_sem, send_sem, recv_sem, zs_sem, zr_sem = scratch[8 + bits :]
    tokens, rows = og.shape
    block = rows // dp
    width = w_hbm.shape[1]
    n, parts = width // CHUNK, width // PART
    share_of = CHUNK // PART
    me, z = lax.axis_index("dp"), lax.axis_index("tensor")

    plane = (bits - 1) // 2
    along_x = list(range(1, 1 + plane))
    along_y = list(range(1 + plane, bits))
    orders = ([0] + along_x + along_y, [0] + along_y + along_x)

    def partner(b):
        mine = bit(me, b)
        return (me + (1 - 2 * mine) * (1 << b), z)

    def cols(j, size=PART):
        return slice(j * size, (j + 1) * size)

    def in_copy(j):
        return pltpu.make_async_copy(
            in_hbm.at[:, cols(j, CHUNK)], ins.at[j % SLOTS], in_sem.at[j % SLOTS]
        )

    def exchange(s, j):
        half = dp >> (s + 1)
        return pltpu.make_async_remote_copy(
            src_ref=acc.at[j, pl.ds(half, half)],
            dst_ref=recv[s].at[j],
            send_sem=send_sem.at[s, j],
            recv_sem=recv_sem.at[s, j],
            device_id=partner(orders[j % 2][s]),
            device_id_type=MESH,
        )

    piece = tokens // PIECES

    def og_copy(p):
        at = slice(p * piece, (p + 1) * piece)
        return pltpu.make_async_copy(og_hbm.at[at], og.at[at], og_sem.at[p])

    for p in range(PIECES):
        og_copy(p).start()
    in_copy(0).start()
    wms_copies = [
        pltpu.make_async_copy(ref, wms.at[i], wms_sem.at[i])
        for i, ref in enumerate((w_hbm, m_hbm, s_hbm))
    ]

    barrier = pltpu.get_barrier_semaphore()
    peers = [lax.rem(z + d, nt) for d in range(1, nt)]
    for b in range(bits):
        pl.semaphore_signal(barrier, inc=1, device_id=partner(b), device_id_type=MESH)
    for peer in peers:
        pl.semaphore_signal(barrier, inc=1, device_id=(me, peer), device_id_type=MESH)

    tile = 256
    place_of = lax.broadcasted_iota(jnp.int32, (tile, tile), 0)
    row_of = lax.broadcasted_iota(jnp.int32, (tile, tile), 1)
    own = place_of // (tile // 2)
    pair = (place_of % (tile // 2)) // block
    core = bit(me, 0)
    wanted = (2 * pair + 1 - core + own * (2 * core - 1)) * block + place_of % block
    select = (wanted == row_of).astype(jnp.bfloat16)
    for p in range(PIECES):
        og_copy(p).wait()
        if p == PIECES - 1:
            for j in range(1, min(SLOTS, n)):
                in_copy(j).start()

        def transpose(r, _, p=p):
            rs = pl.ds(pl.multiple_of(r * tile, tile), tile)
            for k in range(p * piece // tile, (p + 1) * piece // tile):
                ks = slice(k * tile, (k + 1) * tile)
                turned = lax.dot_general(
                    select,
                    og[ks, rs],
                    (((1,), (1,)), ((), ())),
                    preferred_element_type=jnp.float32,
                ).astype(jnp.bfloat16)
                for h in range(2):
                    at = h * (rows // 2) + r * (tile // 2)
                    og_t[pl.ds(pl.multiple_of(at, tile // 2), tile // 2), ks] = turned[
                        h * (tile // 2) : (h + 1) * (tile // 2)
                    ]
            return 0

        lax.fori_loop(0, rows // tile, transpose, 0, unroll=rows <= 2 * tile)

    def multiply(j, size, first, last):
        def group(g, _):
            at = pl.ds(pl.multiple_of(g * size, size), size)
            part = jnp.dot(
                og_t[at, :], ins[j % SLOTS], preferred_element_type=jnp.float32
            )
            for o in range(size // block):
                at = g * (size // block) + o
                for q in range(share_of):
                    place = (1 - at // (dp // 2)) * (dp // 2)
                    for s, b in enumerate(orders[q % 2]):
                        if s:
                            place += lax.rem(bit(me, b) + bit(at, b - 1), 2) * (dp >> (s + 1))
                    acc[j * share_of + q, place] = part[o * block : (o + 1) * block, cols(q)]
            return 0

        lax.fori_loop(first // size, last // size, group, 0)

    def receive(s, j):
        half = dp >> (s + 1)
        exchange(s, j).wait_recv()
        if s < bits - 1:
            acc[j, pl.ds(0, half)] += recv[s][j]
            exchange(s + 1, j).start()
            return
        if j == 0:
            for copy in wms_copies:
                copy.wait()
        grad = acc[j, 0] + recv[s][j, 0]
        moved, new_moment, new_second = finish(
            grad, wms[0, :, cols(j)], wms[1, :, cols(j)], wms[2, :, cols(j)]
        )
        moved_ref[:, cols(j)] = moved
        moment_ref[:, cols(j)] = new_moment
        second_ref[:, cols(j)] = new_second
        square = moved * moved
        tot[...] = square if j == 0 else tot[...] + square

    def each(j, action):
        for q in range(share_of):
            action(j * share_of + q)

    for j in range(n):
        in_copy(j).wait()
        if j < SPLIT:
            multiply(j, GROUP // 2, 0, rows // 2)
            if j == 0:
                pl.semaphore_wait(barrier, bits + nt - 1)
            each(j, lambda q: exchange(0, q).start())
            multiply(j, GROUP // 2, rows // 2, rows)
        else:
            multiply(j, GROUP, 0, rows)
            each(j, lambda q: exchange(0, q).start())
        if j == 0:
            for copy in wms_copies:
                copy.start()
        if j + SLOTS < n:
            in_copy(j + SLOTS).start()
        if j >= 1:
            each(j - 1, lambda q: receive(0, q))
    each(n - 1, lambda q: receive(0, q))
    for i in range(parts + LAG * (bits - 2)):
        for s in range(1, bits):
            j = i - LAG * (s - 1)
            if 0 <= j < parts:
                receive(s, j)

    exact = lax.Precision.HIGHEST
    zsend[...] = lax.dot_general(
        jnp.ones((8, 128), jnp.float32),
        tot[...],
        (((1,), (1,)), ((), ())),
        precision=exact,
        preferred_element_type=jnp.float32,
    )

    def share(d):
        return pltpu.make_async_remote_copy(
            src_ref=zsend,
            dst_ref=zrecv.at[d],
            send_sem=zs_sem.at[d],
            recv_sem=zr_sem.at[d],
            device_id=(me, peers[d]),
            device_id_type=MESH,
        )

    for d in range(nt - 1):
        share(d).start()
    for s in range(bits):
        for j in range(parts):
            exchange(s, j).wait_send()
    for d in range(nt - 1):
        share(d).wait_send()
    total = zsend[...]
    for d in range(nt - 1):
        share(d).wait_recv()
        total = total + zrecv[d]
    row_total = lax.dot_general(
        total,
        jnp.full((8, 128), 0.125, jnp.float32),
        (((0,), (0,)), ((), ())),
        precision=exact,
        preferred_element_type=jnp.float32,
    )
    out_scale[...] = lax.rsqrt(row_total / (width * nt) + 1e-06)


def write_kernel(moved, moment, second, scale, out_w, out_m, out_s, scaled, sem):
    copies = [
        pltpu.make_async_copy(src, dst, sem.at[i])
        for i, (src, dst) in enumerate(((scaled, out_w), (moment, out_m), (second, out_s)))
    ]
    copies[1].start()
    copies[2].start()
    for c in range(moved.shape[1] // 128):
        cs = slice(c * 128, (c + 1) * 128)
        scaled[:, cs] = moved[:, cs] * scale[...]
    copies[0].start()
    for copy in copies:
        copy.wait()


def on_device(dp, nt, out_grad, inputs, weights, moment, second):
    tokens, rows = out_grad.shape
    block, width = weights.shape
    parts = width // PART
    bits = dp.bit_length() - 1
    dma = pltpu.SemaphoreType.DMA
    scratch = [
        pltpu.VMEM((tokens, rows), jnp.bfloat16),
        pltpu.VMEM((rows, tokens), jnp.bfloat16),
        pltpu.VMEM((SLOTS, tokens, CHUNK), jnp.bfloat16),
        pltpu.VMEM((3, block, width), jnp.float32),
        pltpu.VMEM((parts, dp, block, PART), jnp.float32),
        pltpu.VMEM((block, 128), jnp.float32),
        pltpu.VMEM((8, block), jnp.float32),
        pltpu.VMEM((nt - 1, 8, block), jnp.float32),
    ]
    scratch += [
        pltpu.VMEM((parts, dp >> (s + 1), block, PART), jnp.float32) for s in range(bits)
    ]
    scratch += [
        dma((PIECES,)),
        dma((SLOTS,)),
        dma((3,)),
        dma((bits, parts)),
        dma((bits, parts)),
        dma((nt - 1,)),
        dma((nt - 1,)),
    ]
    held = sum(
        jnp.dtype(ref.dtype).itemsize * math.prod(ref.shape)
        for ref in scratch
        if getattr(ref, "memory_space", None) == pltpu.VMEM
    )
    shapes = [weights.shape] * 3 + [(block, 128)]
    results = pl.pallas_call(
        functools.partial(kernel, dp, nt),
        out_shape=[pltpu.VMEM(shape, jnp.float32) for shape in shapes],
        in_specs=[pl.BlockSpec(memory_space=pltpu.HBM)] * 5,
        out_specs=[pl.BlockSpec(memory_space=pltpu.VMEM)] * 4,
        scratch_shapes=scratch,
        compiler_params=pltpu.CompilerParams(
            collective_id=0, has_side_effects=True, vmem_limit_bytes=held + (3 << 20)
        ),
    )(
        *(
            pltpu.with_memory_space_constraint(x, pltpu.HBM)
            for x in (out_grad, inputs, weights, moment, second)
        )
    )
    return pl.pallas_call(
        write_kernel,
        out_shape=[pltpu.HBM(weights.shape, jnp.float32)] * 3,
        in_specs=[pl.BlockSpec(memory_space=pltpu.VMEM)] * 4,
        out_specs=[pl.BlockSpec(memory_space=pltpu.HBM)] * 3,
        scratch_shapes=[pltpu.VMEM(weights.shape, jnp.float32), dma((3,))],
        compiler_params=pltpu.CompilerParams(vmem_limit_bytes=2 << 20),
    )(*results)


def solution(mesh):
    held = P("dp", "tensor")
    return jax.shard_map(
        functools.partial(on_device, mesh.shape["dp"], mesh.shape["tensor"]),
        mesh=mesh,
        in_specs=(P("dp", None), held, held, held, held),
        out_specs=(held, held, held),
        check_vma=False,
    )
```

```python
import functools
import math

import jax
import jax.numpy as jnp
from jax import lax
from jax.experimental import pallas as pl
from jax.experimental.pallas import tpu as pltpu
from jax.sharding import PartitionSpec as P

MESH = pl.DeviceIdType.MESH
CHUNK = 256
PART = 128
SLOTS = 4
GROUP = 512
PIECES = 4
SPLIT = 2


def finish(grad, weights, moment, second):
    new_moment = 0.9 * moment + 0.1 * grad
    new_second = 0.95 * second + 0.05 * grad * grad
    step_size = 0.3 * (new_moment / (1.0 - 0.9**10))
    moved = weights - step_size / (jnp.sqrt(new_second / (1.0 - 0.95**10)) + 1e-08)
    return (moved, new_moment, new_second)


def bit(index, b):
    return lax.rem(index // (1 << b), 2)


def kernel(
    dp, nt, og_hbm, in_hbm, w_hbm, m_hbm, s_hbm, moved_ref, moment_ref, second_ref, out_scale, *scratch
):
    bits = dp.bit_length() - 1
    og, og_t, ins, wms, acc, tot, zsend, zrecv = scratch[:8]
    recv = scratch[8 : 8 + bits]
    og_sem, in_sem, wms_sem, send_sem, recv_sem, zs_sem, zr_sem = scratch[8 + bits :]
    tokens, rows = og.shape
    block = rows // dp
    width = w_hbm.shape[1]
    n, parts = width // CHUNK, width // PART
    share_of = CHUNK // PART
    me, z = lax.axis_index("dp"), lax.axis_index("tensor")

    plane = (bits - 1) // 2
    along_x = list(range(1, 1 + plane))
    along_y = list(range(1 + plane, bits))
    orders = ([0] + along_x + along_y, [0] + along_y + along_x)

    def partner(b):
        mine = bit(me, b)
        return (me + (1 - 2 * mine) * (1 << b), z)

    def cols(j, size=PART):
        return slice(j * size, (j + 1) * size)

    def in_copy(j):
        return pltpu.make_async_copy(
            in_hbm.at[:, cols(j, CHUNK)], ins.at[j % SLOTS], in_sem.at[j % SLOTS]
        )

    def exchange(s, j):
        half = dp >> (s + 1)
        return pltpu.make_async_remote_copy(
            src_ref=acc.at[j, pl.ds(half, half)],
            dst_ref=recv[s].at[j],
            send_sem=send_sem.at[s, j],
            recv_sem=recv_sem.at[s, j],
            device_id=partner(orders[j % 2][s]),
            device_id_type=MESH,
        )

    piece = tokens // PIECES

    def og_copy(p):
        at = slice(p * piece, (p + 1) * piece)
        return pltpu.make_async_copy(og_hbm.at[at], og.at[at], og_sem.at[p])

    for p in range(PIECES):
        og_copy(p).start()
    in_copy(0).start()
    wms_copies = [
        pltpu.make_async_copy(ref, wms.at[i], wms_sem.at[i])
        for i, ref in enumerate((w_hbm, m_hbm, s_hbm))
    ]

    barrier = pltpu.get_barrier_semaphore()
    peers = [lax.rem(z + d, nt) for d in range(1, nt)]
    for b in range(bits):
        pl.semaphore_signal(barrier, inc=1, device_id=partner(b), device_id_type=MESH)
    for peer in peers:
        pl.semaphore_signal(barrier, inc=1, device_id=(me, peer), device_id_type=MESH)

    tile = 256
    place_of = lax.broadcasted_iota(jnp.int32, (tile, tile), 0)
    row_of = lax.broadcasted_iota(jnp.int32, (tile, tile), 1)
    own = place_of // (tile // 2)
    pair = (place_of % (tile // 2)) // block
    core = bit(me, 0)
    wanted = (2 * pair + 1 - core + own * (2 * core - 1)) * block + place_of % block
    select = (wanted == row_of).astype(jnp.bfloat16)
    for p in range(PIECES):
        og_copy(p).wait()
        if p == PIECES - 1:
            for j in range(1, min(SLOTS, n)):
                in_copy(j).start()

        def transpose(r, _, p=p):
            rs = pl.ds(pl.multiple_of(r * tile, tile), tile)
            for k in range(p * piece // tile, (p + 1) * piece // tile):
                ks = slice(k * tile, (k + 1) * tile)
                turned = lax.dot_general(
                    select,
                    og[ks, rs],
                    (((1,), (1,)), ((), ())),
                    preferred_element_type=jnp.float32,
                ).astype(jnp.bfloat16)
                for h in range(2):
                    at = h * (rows // 2) + r * (tile // 2)
                    og_t[pl.ds(pl.multiple_of(at, tile // 2), tile // 2), ks] = turned[
                        h * (tile // 2) : (h + 1) * (tile // 2)
                    ]
            return 0

        lax.fori_loop(0, rows // tile, transpose, 0, unroll=rows <= 2 * tile)

    def multiply(j, size, first, last):
        def group(g, _):
            at = pl.ds(pl.multiple_of(g * size, size), size)
            part = jnp.dot(
                og_t[at, :], ins[j % SLOTS], preferred_element_type=jnp.float32
            )
            for o in range(size // block):
                at = g * (size // block) + o
                for q in range(share_of):
                    place = (1 - at // (dp // 2)) * (dp // 2)
                    for s, b in enumerate(orders[q % 2]):
                        if s:
                            place += lax.rem(bit(me, b) + bit(at, b - 1), 2) * (dp >> (s + 1))
                    acc[j * share_of + q, place] = part[o * block : (o + 1) * block, cols(q)]
            return 0

        lax.fori_loop(first // size, last // size, group, 0)

    def receive(s, j):
        half = dp >> (s + 1)
        exchange(s, j).wait_recv()
        if s < bits - 1:
            acc[j, pl.ds(0, half)] += recv[s][j]
            exchange(s + 1, j).start()
            return
        if j == 0:
            for copy in wms_copies:
                copy.wait()
        grad = acc[j, 0] + recv[s][j, 0]
        moved, new_moment, new_second = finish(
            grad, wms[0, :, cols(j)], wms[1, :, cols(j)], wms[2, :, cols(j)]
        )
        moved_ref[:, cols(j)] = moved
        moment_ref[:, cols(j)] = new_moment
        second_ref[:, cols(j)] = new_second
        square = moved * moved
        tot[...] = square if j == 0 else tot[...] + square

    def each(j, action):
        for q in range(share_of):
            action(j * share_of + q)

    for j in range(n):
        in_copy(j).wait()
        if j < SPLIT:
            multiply(j, GROUP // 2, 0, rows // 2)
            if j == 0:
                pl.semaphore_wait(barrier, bits + nt - 1)
            each(j, lambda q: exchange(0, q).start())
            if j:
                each(j - 1, lambda q: receive(0, q))
            multiply(j, GROUP // 2, rows // 2, rows)
        else:
            multiply(j, GROUP, 0, rows)
            each(j, lambda q: exchange(0, q).start())
            each(j - 1, lambda q: receive(0, q))
        if j == 0:
            for copy in wms_copies:
                copy.start()
        if j + SLOTS < n:
            in_copy(j + SLOTS).start()
    each(n - 1, lambda q: receive(0, q))
    for s in range(1, bits):
        for j in range(parts):
            receive(s, j)

    exact = lax.Precision.HIGHEST
    zsend[...] = lax.dot_general(
        jnp.ones((8, 128), jnp.float32),
        tot[...],
        (((1,), (1,)), ((), ())),
        precision=exact,
        preferred_element_type=jnp.float32,
    )

    def share(d):
        return pltpu.make_async_remote_copy(
            src_ref=zsend,
            dst_ref=zrecv.at[d],
            send_sem=zs_sem.at[d],
            recv_sem=zr_sem.at[d],
            device_id=(me, peers[d]),
            device_id_type=MESH,
        )

    for d in range(nt - 1):
        share(d).start()
    for s in range(bits):
        for j in range(parts):
            exchange(s, j).wait_send()
    for d in range(nt - 1):
        share(d).wait_send()
    total = zsend[...]
    for d in range(nt - 1):
        share(d).wait_recv()
        total = total + zrecv[d]
    row_total = lax.dot_general(
        total,
        jnp.full((8, 128), 0.125, jnp.float32),
        (((0,), (0,)), ((), ())),
        precision=exact,
        preferred_element_type=jnp.float32,
    )
    out_scale[...] = lax.rsqrt(row_total / (width * nt) + 1e-06)


def write_kernel(moved, moment, second, scale, out_w, out_m, out_s, scaled, sem):
    copies = [
        pltpu.make_async_copy(src, dst, sem.at[i])
        for i, (src, dst) in enumerate(((scaled, out_w), (moment, out_m), (second, out_s)))
    ]
    copies[1].start()
    copies[2].start()
    for c in range(moved.shape[1] // 128):
        cs = slice(c * 128, (c + 1) * 128)
        scaled[:, cs] = moved[:, cs] * scale[...]
    copies[0].start()
    for copy in copies:
        copy.wait()


def on_device(dp, nt, out_grad, inputs, weights, moment, second):
    tokens, rows = out_grad.shape
    block, width = weights.shape
    parts = width // PART
    bits = dp.bit_length() - 1
    dma = pltpu.SemaphoreType.DMA
    scratch = [
        pltpu.VMEM((tokens, rows), jnp.bfloat16),
        pltpu.VMEM((rows, tokens), jnp.bfloat16),
        pltpu.VMEM((SLOTS, tokens, CHUNK), jnp.bfloat16),
        pltpu.VMEM((3, block, width), jnp.float32),
        pltpu.VMEM((parts, dp, block, PART), jnp.float32),
        pltpu.VMEM((block, 128), jnp.float32),
        pltpu.VMEM((8, block), jnp.float32),
        pltpu.VMEM((nt - 1, 8, block), jnp.float32),
    ]
    scratch += [
        pltpu.VMEM((parts, dp >> (s + 1), block, PART), jnp.float32) for s in range(bits)
    ]
    scratch += [
        dma((PIECES,)),
        dma((SLOTS,)),
        dma((3,)),
        dma((bits, parts)),
        dma((bits, parts)),
        dma((nt - 1,)),
        dma((nt - 1,)),
    ]
    held = sum(
        jnp.dtype(ref.dtype).itemsize * math.prod(ref.shape)
        for ref in scratch
        if getattr(ref, "memory_space", None) == pltpu.VMEM
    )
    shapes = [weights.shape] * 3 + [(block, 128)]
    results = pl.pallas_call(
        functools.partial(kernel, dp, nt),
        out_shape=[pltpu.VMEM(shape, jnp.float32) for shape in shapes],
        in_specs=[pl.BlockSpec(memory_space=pltpu.HBM)] * 5,
        out_specs=[pl.BlockSpec(memory_space=pltpu.VMEM)] * 4,
        scratch_shapes=scratch,
        compiler_params=pltpu.CompilerParams(
            collective_id=0, has_side_effects=True, vmem_limit_bytes=held + (3 << 20)
        ),
    )(
        *(
            pltpu.with_memory_space_constraint(x, pltpu.HBM)
            for x in (out_grad, inputs, weights, moment, second)
        )
    )
    return pl.pallas_call(
        write_kernel,
        out_shape=[pltpu.HBM(weights.shape, jnp.float32)] * 3,
        in_specs=[pl.BlockSpec(memory_space=pltpu.VMEM)] * 4,
        out_specs=[pl.BlockSpec(memory_space=pltpu.HBM)] * 3,
        scratch_shapes=[pltpu.VMEM(weights.shape, jnp.float32), dma((3,))],
        compiler_params=pltpu.CompilerParams(vmem_limit_bytes=2 << 20),
    )(*results)


def solution(mesh):
    held = P("dp", "tensor")
    return jax.shard_map(
        functools.partial(on_device, mesh.shape["dp"], mesh.shape["tensor"]),
        mesh=mesh,
        in_specs=(P("dp", None), held, held, held, held),
        out_specs=(held, held, held),
        check_vma=False,
    )
```

```python
import functools
import math

import jax
import jax.numpy as jnp
from jax import lax
from jax.experimental import pallas as pl
from jax.experimental.pallas import tpu as pltpu
from jax.sharding import PartitionSpec as P

MESH = pl.DeviceIdType.MESH
CHUNK = 256
PART = 128
SLOTS = 4
GROUP = 512
PIECES = 4
AHEAD = 5
SPLIT = 2


def finish(grad, weights, moment, second):
    new_moment = 0.9 * moment + 0.1 * grad
    new_second = 0.95 * second + 0.05 * grad * grad
    step_size = 0.3 * (new_moment / (1.0 - 0.9**10))
    moved = weights - step_size / (jnp.sqrt(new_second / (1.0 - 0.95**10)) + 1e-08)
    return (moved, new_moment, new_second)


def bit(index, b):
    return lax.rem(index // (1 << b), 2)


def kernel(
    dp, nt, og_hbm, in_hbm, w_hbm, m_hbm, s_hbm, moved_ref, moment_ref, second_ref, out_scale, *scratch
):
    bits = dp.bit_length() - 1
    og, og_t, ins, wms, acc, tot, zsend, zrecv = scratch[:8]
    recv = scratch[8 : 8 + bits]
    og_sem, in_sem, wms_sem, send_sem, recv_sem, zs_sem, zr_sem = scratch[8 + bits :]
    tokens, rows = og.shape
    block = rows // dp
    width = w_hbm.shape[1]
    n, parts = width // CHUNK, width // PART
    share_of = CHUNK // PART
    me, z = lax.axis_index("dp"), lax.axis_index("tensor")

    plane = (bits - 1) // 2
    along_x = list(range(1, 1 + plane))
    along_y = list(range(1 + plane, bits))
    orders = ([0] + along_x + along_y, [0] + along_y + along_x)

    def partner(b):
        mine = bit(me, b)
        return (me + (1 - 2 * mine) * (1 << b), z)

    def cols(j, size=PART):
        return slice(j * size, (j + 1) * size)

    def in_copy(j):
        return pltpu.make_async_copy(
            in_hbm.at[:, cols(j, CHUNK)], ins.at[j % SLOTS], in_sem.at[j % SLOTS]
        )

    def exchange(s, j):
        half = dp >> (s + 1)
        return pltpu.make_async_remote_copy(
            src_ref=acc.at[j, pl.ds(half, half)],
            dst_ref=recv[s].at[j],
            send_sem=send_sem.at[s, j],
            recv_sem=recv_sem.at[s, j],
            device_id=partner(orders[j % 2][s]),
            device_id_type=MESH,
        )

    piece = tokens // PIECES

    def og_copy(p):
        at = slice(p * piece, (p + 1) * piece)
        return pltpu.make_async_copy(og_hbm.at[at], og.at[at], og_sem.at[p])

    for p in range(PIECES):
        og_copy(p).start()
    in_copy(0).start()
    wms_copies = [
        pltpu.make_async_copy(ref, wms.at[i], wms_sem.at[i])
        for i, ref in enumerate((w_hbm, m_hbm, s_hbm))
    ]

    barrier = pltpu.get_barrier_semaphore()
    peers = [lax.rem(z + d, nt) for d in range(1, nt)]
    for b in range(bits):
        pl.semaphore_signal(barrier, inc=1, device_id=partner(b), device_id_type=MESH)
    for peer in peers:
        pl.semaphore_signal(barrier, inc=1, device_id=(me, peer), device_id_type=MESH)

    tile = 256
    place_of = lax.broadcasted_iota(jnp.int32, (tile, tile), 0)
    row_of = lax.broadcasted_iota(jnp.int32, (tile, tile), 1)
    own = place_of // (tile // 2)
    pair = (place_of % (tile // 2)) // block
    core = bit(me, 0)
    wanted = (2 * pair + 1 - core + own * (2 * core - 1)) * block + place_of % block
    select = (wanted == row_of).astype(jnp.bfloat16)
    for p in range(PIECES):
        og_copy(p).wait()
        if p == PIECES - 1:
            for j in range(1, min(SLOTS, n)):
                in_copy(j).start()

        def transpose(r, _, p=p):
            rs = pl.ds(pl.multiple_of(r * tile, tile), tile)
            for k in range(p * piece // tile, (p + 1) * piece // tile):
                ks = slice(k * tile, (k + 1) * tile)
                turned = lax.dot_general(
                    select,
                    og[ks, rs],
                    (((1,), (1,)), ((), ())),
                    preferred_element_type=jnp.float32,
                ).astype(jnp.bfloat16)
                for h in range(2):
                    at = h * (rows // 2) + r * (tile // 2)
                    og_t[pl.ds(pl.multiple_of(at, tile // 2), tile // 2), ks] = turned[
                        h * (tile // 2) : (h + 1) * (tile // 2)
                    ]
            return 0

        lax.fori_loop(0, rows // tile, transpose, 0, unroll=rows <= 2 * tile)

    def multiply(j, size, first, last):
        def group(g, _):
            at = pl.ds(pl.multiple_of(g * size, size), size)
            part = jnp.dot(
                og_t[at, :], ins[j % SLOTS], preferred_element_type=jnp.float32
            )
            for o in range(size // block):
                at = g * (size // block) + o
                for q in range(share_of):
                    place = (1 - at // (dp // 2)) * (dp // 2)
                    for s, b in enumerate(orders[q % 2]):
                        if s:
                            place += lax.rem(bit(me, b) + bit(at, b - 1), 2) * (dp >> (s + 1))
                    acc[j * share_of + q, place] = part[o * block : (o + 1) * block, cols(q)]
            return 0

        lax.fori_loop(first // size, last // size, group, 0)

    def receive(s, j):
        half = dp >> (s + 1)
        exchange(s, j).wait_recv()
        if s < bits - 1:
            acc[j, pl.ds(0, half)] += recv[s][j]
            exchange(s + 1, j).start()
            return
        if j == 0:
            for copy in wms_copies:
                copy.wait()
        grad = acc[j, 0] + recv[s][j, 0]
        moved, new_moment, new_second = finish(
            grad, wms[0, :, cols(j)], wms[1, :, cols(j)], wms[2, :, cols(j)]
        )
        moved_ref[:, cols(j)] = moved
        moment_ref[:, cols(j)] = new_moment
        second_ref[:, cols(j)] = new_second
        square = moved * moved
        tot[...] = square if j == 0 else tot[...] + square

    def each(j, action):
        for q in range(share_of):
            action(j * share_of + q)

    for j in range(n):
        in_copy(j).wait()
        if j < SPLIT:
            multiply(j, GROUP // 2, 0, rows // 2)
            if j == 0:
                pl.semaphore_wait(barrier, bits + nt - 1)
            each(j, lambda q: exchange(0, q).start())
            if j:
                each(j - 1, lambda q: receive(0, q))
            multiply(j, GROUP // 2, rows // 2, rows)
        else:
            multiply(j, GROUP, 0, rows)
            each(j, lambda q: exchange(0, q).start())
            each(j - 1, lambda q: receive(0, q))
        if j >= AHEAD:
            each(j - AHEAD, lambda q: receive(1, q))
        if j == 0:
            for copy in wms_copies:
                copy.start()
        if j + SLOTS < n:
            in_copy(j + SLOTS).start()
    each(n - 1, lambda q: receive(0, q))
    for s in range(1, bits):
        for j in range(max(n - AHEAD, 0) * share_of if s == 1 else 0, parts):
            receive(s, j)

    def pair_of(value, axis):
        high = value.astype(jnp.bfloat16)
        rest = (value - high.astype(jnp.float32)).astype(jnp.bfloat16)
        return jnp.concatenate([high, rest], axis=axis)

    zsend[...] = lax.dot_general(
        jnp.ones((8, 256), jnp.bfloat16),
        pair_of(tot[...], 1),
        (((1,), (1,)), ((), ())),
        preferred_element_type=jnp.float32,
    )

    def share(d):
        return pltpu.make_async_remote_copy(
            src_ref=zsend,
            dst_ref=zrecv.at[d],
            send_sem=zs_sem.at[d],
            recv_sem=zr_sem.at[d],
            device_id=(me, peers[d]),
            device_id_type=MESH,
        )

    for d in range(nt - 1):
        share(d).start()
    for s in range(bits):
        for j in range(parts):
            exchange(s, j).wait_send()
    for d in range(nt - 1):
        share(d).wait_send()
    total = zsend[...]
    for d in range(nt - 1):
        share(d).wait_recv()
        total = total + zrecv[d]
    row_total = lax.dot_general(
        pair_of(total, 0),
        jnp.full((16, 128), 0.125, jnp.bfloat16),
        (((0,), (0,)), ((), ())),
        preferred_element_type=jnp.float32,
    )
    out_scale[...] = lax.rsqrt(row_total / (width * nt) + 1e-06)


def write_kernel(moved, moment, second, scale, out_w, out_m, out_s, scaled, sem):
    copies = [
        pltpu.make_async_copy(src, dst, sem.at[i])
        for i, (src, dst) in enumerate(((scaled, out_w), (moment, out_m), (second, out_s)))
    ]
    copies[1].start()
    copies[2].start()
    for c in range(moved.shape[1] // 128):
        cs = slice(c * 128, (c + 1) * 128)
        scaled[:, cs] = moved[:, cs] * scale[...]
    copies[0].start()
    for copy in copies:
        copy.wait()


def on_device(dp, nt, out_grad, inputs, weights, moment, second):
    tokens, rows = out_grad.shape
    block, width = weights.shape
    parts = width // PART
    bits = dp.bit_length() - 1
    dma = pltpu.SemaphoreType.DMA
    scratch = [
        pltpu.VMEM((tokens, rows), jnp.bfloat16),
        pltpu.VMEM((rows, tokens), jnp.bfloat16),
        pltpu.VMEM((SLOTS, tokens, CHUNK), jnp.bfloat16),
        pltpu.VMEM((3, block, width), jnp.float32),
        pltpu.VMEM((parts, dp, block, PART), jnp.float32),
        pltpu.VMEM((block, 128), jnp.float32),
        pltpu.VMEM((8, block), jnp.float32),
        pltpu.VMEM((nt - 1, 8, block), jnp.float32),
    ]
    scratch += [
        pltpu.VMEM((parts, dp >> (s + 1), block, PART), jnp.float32) for s in range(bits)
    ]
    scratch += [
        dma((PIECES,)),
        dma((SLOTS,)),
        dma((3,)),
        dma((bits, parts)),
        dma((bits, parts)),
        dma((nt - 1,)),
        dma((nt - 1,)),
    ]
    held = sum(
        jnp.dtype(ref.dtype).itemsize * math.prod(ref.shape)
        for ref in scratch
        if getattr(ref, "memory_space", None) == pltpu.VMEM
    )
    shapes = [weights.shape] * 3 + [(block, 128)]
    results = pl.pallas_call(
        functools.partial(kernel, dp, nt),
        out_shape=[pltpu.VMEM(shape, jnp.float32) for shape in shapes],
        in_specs=[pl.BlockSpec(memory_space=pltpu.HBM)] * 5,
        out_specs=[pl.BlockSpec(memory_space=pltpu.VMEM)] * 4,
        scratch_shapes=scratch,
        compiler_params=pltpu.CompilerParams(
            collective_id=0, has_side_effects=True, vmem_limit_bytes=held + (3 << 20)
        ),
    )(
        *(
            pltpu.with_memory_space_constraint(x, pltpu.HBM)
            for x in (out_grad, inputs, weights, moment, second)
        )
    )
    return pl.pallas_call(
        write_kernel,
        out_shape=[pltpu.HBM(weights.shape, jnp.float32)] * 3,
        in_specs=[pl.BlockSpec(memory_space=pltpu.VMEM)] * 4,
        out_specs=[pl.BlockSpec(memory_space=pltpu.HBM)] * 3,
        scratch_shapes=[pltpu.VMEM(weights.shape, jnp.float32), dma((3,))],
        compiler_params=pltpu.CompilerParams(vmem_limit_bytes=2 << 20),
    )(*results)


def solution(mesh):
    held = P("dp", "tensor")
    return jax.shard_map(
        functools.partial(on_device, mesh.shape["dp"], mesh.shape["tensor"]),
        mesh=mesh,
        in_specs=(P("dp", None), held, held, held, held),
        out_specs=(held, held, held),
        check_vma=False,
    )
```

```python
import functools
import math

import jax
import jax.numpy as jnp
from jax import lax
from jax.experimental import pallas as pl
from jax.experimental.pallas import tpu as pltpu
from jax.sharding import PartitionSpec as P

MESH = pl.DeviceIdType.MESH
CHUNK = 256
PART = 128
SLOTS = 4
GROUP = 512
PIECES = 4
AHEAD = 5
SPLIT = 2


def finish(grad, weights, moment, second):
    new_moment = 0.9 * moment + 0.1 * grad
    new_second = 0.95 * second + 0.05 * grad * grad
    step_size = 0.3 * (new_moment / (1.0 - 0.9**10))
    moved = weights - step_size / (jnp.sqrt(new_second / (1.0 - 0.95**10)) + 1e-08)
    return (moved, new_moment, new_second)


def bit(index, b):
    return lax.rem(index // (1 << b), 2)


def kernel(
    dp, nt, og_hbm, in_hbm, w_hbm, m_hbm, s_hbm, moved_ref, moment_ref, second_ref, out_scale, *scratch
):
    bits = dp.bit_length() - 1
    og, og_t, ins, wms, acc, tot, zsend, zrecv = scratch[:8]
    recv = scratch[8 : 8 + bits]
    og_sem, in_sem, wms_sem, send_sem, recv_sem, zs_sem, zr_sem = scratch[8 + bits :]
    tokens, rows = og.shape
    block = rows // dp
    width = w_hbm.shape[1]
    n, parts = width // CHUNK, width // PART
    share_of = CHUNK // PART
    me, z = lax.axis_index("dp"), lax.axis_index("tensor")

    plane = (bits - 1) // 2
    along_x = list(range(1, 1 + plane))
    along_y = list(range(1 + plane, bits))
    orders = ([0] + along_x + along_y, [0] + along_y + along_x)

    def partner(b):
        mine = bit(me, b)
        return (me + (1 - 2 * mine) * (1 << b), z)

    def cols(j, size=PART):
        return slice(j * size, (j + 1) * size)

    def in_copy(j):
        return pltpu.make_async_copy(
            in_hbm.at[:, cols(j, CHUNK)], ins.at[j % SLOTS], in_sem.at[j % SLOTS]
        )

    def swap(j):
        return pltpu.make_async_remote_copy(
            src_ref=acc.at[j, 1],
            dst_ref=recv[0].at[j],
            send_sem=send_sem.at[0, j],
            recv_sem=recv_sem.at[0, j],
            device_id=partner(0),
            device_id_type=MESH,
        )

    def exchange(s, j):
        half = dp >> (s + 1)
        return pltpu.make_async_remote_copy(
            src_ref=acc.at[j // share_of, 0, j % share_of, pl.ds(half, half)],
            dst_ref=recv[s].at[j],
            send_sem=send_sem.at[s, j],
            recv_sem=recv_sem.at[s, j],
            device_id=partner(orders[j % 2][s]),
            device_id_type=MESH,
        )

    piece = tokens // PIECES

    def og_copy(p):
        at = slice(p * piece, (p + 1) * piece)
        return pltpu.make_async_copy(og_hbm.at[at], og.at[at], og_sem.at[p])

    for p in range(PIECES):
        og_copy(p).start()
    in_copy(0).start()
    wms_copies = [
        pltpu.make_async_copy(ref, wms.at[i], wms_sem.at[i])
        for i, ref in enumerate((w_hbm, m_hbm, s_hbm))
    ]

    barrier = pltpu.get_barrier_semaphore()
    peers = [lax.rem(z + d, nt) for d in range(1, nt)]
    for b in range(bits):
        pl.semaphore_signal(barrier, inc=1, device_id=partner(b), device_id_type=MESH)
    for peer in peers:
        pl.semaphore_signal(barrier, inc=1, device_id=(me, peer), device_id_type=MESH)

    tile = 256
    place_of = lax.broadcasted_iota(jnp.int32, (tile, tile), 0)
    row_of = lax.broadcasted_iota(jnp.int32, (tile, tile), 1)
    own = place_of // (tile // 2)
    pair = (place_of % (tile // 2)) // block
    core = bit(me, 0)
    wanted = (2 * pair + 1 - core + own * (2 * core - 1)) * block + place_of % block
    select = (wanted == row_of).astype(jnp.bfloat16)
    for p in range(PIECES):
        og_copy(p).wait()
        if p == PIECES - 1:
            for j in range(1, min(SLOTS, n)):
                in_copy(j).start()

        def transpose(r, _, p=p):
            rs = pl.ds(pl.multiple_of(r * tile, tile), tile)
            for k in range(p * piece // tile, (p + 1) * piece // tile):
                ks = slice(k * tile, (k + 1) * tile)
                if k % 2:
                    turned = jnp.transpose(og[ks, rs])
                    for o in range(tile // block):
                        h = 1 - lax.rem(core + o, 2)
                        at = h * (rows // 2) + r * (tile // 2) + (o // 2) * block
                        og_t[pl.ds(pl.multiple_of(at, block), block), ks] = turned[
                            o * block : (o + 1) * block
                        ]
                    continue
                turned = lax.dot_general(
                    select,
                    og[ks, rs],
                    (((1,), (1,)), ((), ())),
                    preferred_element_type=jnp.float32,
                ).astype(jnp.bfloat16)
                for h in range(2):
                    at = h * (rows // 2) + r * (tile // 2)
                    og_t[pl.ds(pl.multiple_of(at, tile // 2), tile // 2), ks] = turned[
                        h * (tile // 2) : (h + 1) * (tile // 2)
                    ]
            return 0

        lax.fori_loop(0, rows // tile, transpose, 0, unroll=rows <= 2 * tile)

    def multiply(j, size, first, last):
        def group(g, _):
            at = pl.ds(pl.multiple_of(g * size, size), size)
            part = jnp.dot(
                og_t[at, :], ins[j % SLOTS], preferred_element_type=jnp.float32
            )
            for o in range(size // block):
                at = g * (size // block) + o
                for q in range(share_of):
                    place = 0
                    for s, b in enumerate(orders[q % 2]):
                        if s:
                            place += lax.rem(bit(me, b) + bit(at, b - 1), 2) * (dp >> (s + 1))
                    acc[j, 1 - at // (dp // 2), q, place] = part[o * block : (o + 1) * block, cols(q)]
            return 0

        lax.fori_loop(first // size, last // size, group, 0)

    def receive(s, j):
        half = dp >> (s + 1)
        held = (j // share_of, 0, j % share_of)
        exchange(s, j).wait_recv()
        if s < bits - 1:
            acc[(*held, pl.ds(0, half))] += recv[s][j]
            exchange(s + 1, j).start()
            return
        if j == 0:
            for copy in wms_copies:
                copy.wait()
        grad = acc[(*held, 0)] + recv[s][j, 0]
        moved, new_moment, new_second = finish(
            grad, wms[0, :, cols(j)], wms[1, :, cols(j)], wms[2, :, cols(j)]
        )
        moved_ref[:, cols(j)] = moved
        moment_ref[:, cols(j)] = new_moment
        second_ref[:, cols(j)] = new_second
        square = moved * moved
        tot[...] = square if j == 0 else tot[...] + square

    def sum_cores(j):
        swap(j).wait_recv()
        for q in range(share_of):
            acc[j, 0, q] += recv[0][j, q]
            exchange(1, j * share_of + q).start()

    def each(j, action):
        for q in range(share_of):
            action(j * share_of + q)

    for j in range(n):
        in_copy(j).wait()
        if j < SPLIT:
            multiply(j, GROUP // 2, 0, rows // 2)
            if j == 0:
                pl.semaphore_wait(barrier, bits + nt - 1)
            swap(j).start()
            if j:
                sum_cores(j - 1)
            multiply(j, GROUP // 2, rows // 2, rows)
        else:
            multiply(j, GROUP, 0, rows)
            swap(j).start()
            sum_cores(j - 1)
        if j >= AHEAD:
            each(j - AHEAD, lambda q: receive(1, q))
        if j == 0:
            for copy in wms_copies:
                copy.start()
        if j + SLOTS < n:
            in_copy(j + SLOTS).start()
    sum_cores(n - 1)
    for s in range(1, bits):
        for j in range(max(n - AHEAD, 0) * share_of if s == 1 else 0, parts):
            receive(s, j)

    def pair_of(value, axis):
        high = value.astype(jnp.bfloat16)
        rest = (value - high.astype(jnp.float32)).astype(jnp.bfloat16)
        return jnp.concatenate([high, rest], axis=axis)

    zsend[...] = lax.dot_general(
        jnp.ones((8, 256), jnp.bfloat16),
        pair_of(tot[...], 1),
        (((1,), (1,)), ((), ())),
        preferred_element_type=jnp.float32,
    )

    def share(d):
        return pltpu.make_async_remote_copy(
            src_ref=zsend,
            dst_ref=zrecv.at[d],
            send_sem=zs_sem.at[d],
            recv_sem=zr_sem.at[d],
            device_id=(me, peers[d]),
            device_id_type=MESH,
        )

    for d in range(nt - 1):
        share(d).start()
    for j in range(n):
        swap(j).wait_send()
    for s in range(1, bits):
        for j in range(parts):
            exchange(s, j).wait_send()
    for d in range(nt - 1):
        share(d).wait_send()
    total = zsend[...]
    for d in range(nt - 1):
        share(d).wait_recv()
        total = total + zrecv[d]
    row_total = lax.dot_general(
        pair_of(total, 0),
        jnp.full((16, 128), 0.125, jnp.bfloat16),
        (((0,), (0,)), ((), ())),
        preferred_element_type=jnp.float32,
    )
    out_scale[...] = lax.rsqrt(row_total / (width * nt) + 1e-06)


def write_kernel(moved, moment, second, scale, out_w, out_m, out_s, scaled, sem):
    copies = [
        pltpu.make_async_copy(src, dst, sem.at[i])
        for i, (src, dst) in enumerate(((scaled, out_w), (moment, out_m), (second, out_s)))
    ]
    copies[1].start()
    copies[2].start()
    for c in range(moved.shape[1] // 128):
        cs = slice(c * 128, (c + 1) * 128)
        scaled[:, cs] = moved[:, cs] * scale[...]
    copies[0].start()
    for copy in copies:
        copy.wait()


def on_device(dp, nt, out_grad, inputs, weights, moment, second):
    tokens, rows = out_grad.shape
    block, width = weights.shape
    parts = width // PART
    bits = dp.bit_length() - 1
    dma = pltpu.SemaphoreType.DMA
    scratch = [
        pltpu.VMEM((tokens, rows), jnp.bfloat16),
        pltpu.VMEM((rows, tokens), jnp.bfloat16),
        pltpu.VMEM((SLOTS, tokens, CHUNK), jnp.bfloat16),
        pltpu.VMEM((3, block, width), jnp.float32),
        pltpu.VMEM((width // CHUNK, 2, CHUNK // PART, dp // 2, block, PART), jnp.float32),
        pltpu.VMEM((block, 128), jnp.float32),
        pltpu.VMEM((8, block), jnp.float32),
        pltpu.VMEM((nt - 1, 8, block), jnp.float32),
    ]
    scratch += [
        pltpu.VMEM((width // CHUNK, CHUNK // PART, dp // 2, block, PART), jnp.float32)
    ]
    scratch += [
        pltpu.VMEM((parts, dp >> (s + 1), block, PART), jnp.float32) for s in range(1, bits)
    ]
    scratch += [
        dma((PIECES,)),
        dma((SLOTS,)),
        dma((3,)),
        dma((bits, parts)),
        dma((bits, parts)),
        dma((nt - 1,)),
        dma((nt - 1,)),
    ]
    held = sum(
        jnp.dtype(ref.dtype).itemsize * math.prod(ref.shape)
        for ref in scratch
        if getattr(ref, "memory_space", None) == pltpu.VMEM
    )
    shapes = [weights.shape] * 3 + [(block, 128)]
    results = pl.pallas_call(
        functools.partial(kernel, dp, nt),
        out_shape=[pltpu.VMEM(shape, jnp.float32) for shape in shapes],
        in_specs=[pl.BlockSpec(memory_space=pltpu.HBM)] * 5,
        out_specs=[pl.BlockSpec(memory_space=pltpu.VMEM)] * 4,
        scratch_shapes=scratch,
        compiler_params=pltpu.CompilerParams(
            collective_id=0, has_side_effects=True, vmem_limit_bytes=held + (3 << 20)
        ),
    )(
        *(
            pltpu.with_memory_space_constraint(x, pltpu.HBM)
            for x in (out_grad, inputs, weights, moment, second)
        )
    )
    return pl.pallas_call(
        write_kernel,
        out_shape=[pltpu.HBM(weights.shape, jnp.float32)] * 3,
        in_specs=[pl.BlockSpec(memory_space=pltpu.VMEM)] * 4,
        out_specs=[pl.BlockSpec(memory_space=pltpu.HBM)] * 3,
        scratch_shapes=[pltpu.VMEM(weights.shape, jnp.float32), dma((3,))],
        compiler_params=pltpu.CompilerParams(vmem_limit_bytes=2 << 20),
    )(*results)


def solution(mesh):
    held = P("dp", "tensor")
    return jax.shard_map(
        functools.partial(on_device, mesh.shape["dp"], mesh.shape["tensor"]),
        mesh=mesh,
        in_specs=(P("dp", None), held, held, held, held),
        out_specs=(held, held, held),
        check_vma=False,
    )
```

```python
import functools
import math

import jax
import jax.numpy as jnp
from jax import lax
from jax.experimental import pallas as pl
from jax.experimental.pallas import tpu as pltpu
from jax.sharding import PartitionSpec as P

MESH = pl.DeviceIdType.MESH
CHUNK = 256
PART = 128
SLOTS = 4
GROUP = 512
PIECES = 4
AHEAD = 5
SPLIT = 2


def finish(grad, weights, moment, second):
    new_moment = 0.9 * moment + 0.1 * grad
    new_second = 0.95 * second + 0.05 * grad * grad
    step_size = 0.3 * (new_moment / (1.0 - 0.9**10))
    moved = weights - step_size / (jnp.sqrt(new_second / (1.0 - 0.95**10)) + 1e-08)
    return (moved, new_moment, new_second)


def bit(index, b):
    return lax.rem(index // (1 << b), 2)


def kernel(
    dp, nt, og_hbm, in_hbm, w_hbm, m_hbm, s_hbm, moved_ref, moment_ref, second_ref, out_scale, *scratch
):
    bits = dp.bit_length() - 1
    og, og_t, ins, wms, acc, tot, zsend, zrecv = scratch[:8]
    recv = scratch[8 : 8 + bits]
    og_sem, in_sem, wms_sem, send_sem, recv_sem, zs_sem, zr_sem = scratch[8 + bits :]
    tokens, rows = og.shape
    block = rows // dp
    width = w_hbm.shape[1]
    n, parts = width // CHUNK, width // PART
    share_of = CHUNK // PART
    me, z = lax.axis_index("dp"), lax.axis_index("tensor")
    core = bit(me, 0)

    plane = (bits - 1) // 2
    along_x = list(range(1, 1 + plane))
    along_y = list(range(1 + plane, bits))
    orders = ([0] + along_x + along_y, [0] + along_y + along_x)

    def partner(b):
        mine = bit(me, b)
        return (me + (1 - 2 * mine) * (1 << b), z)

    def cols(j, size=PART):
        return slice(j * size, (j + 1) * size)

    def in_copy(j):
        return pltpu.make_async_copy(
            in_hbm.at[:, cols(j, CHUNK)], ins.at[j % SLOTS], in_sem.at[j % SLOTS]
        )

    def chosen(j, core, pair):
        return pair[0] + lax.rem(j % 2 + core, 2) * (pair[1] - pair[0])

    def swap(j):
        return pltpu.make_async_remote_copy(
            src_ref=acc.at[j, 1],
            dst_ref=recv[0].at[j],
            send_sem=send_sem.at[0, j],
            recv_sem=recv_sem.at[0, j],
            device_id=partner(0),
            device_id_type=MESH,
        )

    def exchange(s, j):
        half = dp >> (s + 1)
        return pltpu.make_async_remote_copy(
            src_ref=acc.at[j // share_of, 0, j % share_of, pl.ds(half, half)],
            dst_ref=recv[s].at[j],
            send_sem=send_sem.at[s, j],
            recv_sem=recv_sem.at[s, j],
            device_id=(chosen(j, core, [partner(order[s])[0] for order in orders]), z),
            device_id_type=MESH,
        )

    piece = tokens // PIECES

    def og_copy(p):
        at = slice(p * piece, (p + 1) * piece)
        return pltpu.make_async_copy(og_hbm.at[at], og.at[at], og_sem.at[p])

    for p in range(PIECES):
        og_copy(p).start()
    in_copy(0).start()
    wms_copies = [
        pltpu.make_async_copy(ref, wms.at[i], wms_sem.at[i])
        for i, ref in enumerate((w_hbm, m_hbm, s_hbm))
    ]

    barrier = pltpu.get_barrier_semaphore()
    peers = [lax.rem(z + d, nt) for d in range(1, nt)]
    for b in range(bits):
        pl.semaphore_signal(barrier, inc=1, device_id=partner(b), device_id_type=MESH)
    for peer in peers:
        pl.semaphore_signal(barrier, inc=1, device_id=(me, peer), device_id_type=MESH)

    tile = 256
    place_of = lax.broadcasted_iota(jnp.int32, (tile, tile), 0)
    row_of = lax.broadcasted_iota(jnp.int32, (tile, tile), 1)
    own = place_of // (tile // 2)
    pair = (place_of % (tile // 2)) // block
    wanted = (2 * pair + 1 - core + own * (2 * core - 1)) * block + place_of % block
    select = (wanted == row_of).astype(jnp.bfloat16)
    for p in range(PIECES):
        og_copy(p).wait()
        if p == PIECES - 1:
            for j in range(1, min(SLOTS, n)):
                in_copy(j).start()

        def transpose(r, _, p=p):
            rs = pl.ds(pl.multiple_of(r * tile, tile), tile)
            for k in range(p * piece // tile, (p + 1) * piece // tile):
                ks = slice(k * tile, (k + 1) * tile)
                if k % 2:
                    turned = jnp.transpose(og[ks, rs])
                    for o in range(tile // block):
                        h = 1 - lax.rem(core + o, 2)
                        at = h * (rows // 2) + r * (tile // 2) + (o // 2) * block
                        og_t[pl.ds(pl.multiple_of(at, block), block), ks] = turned[
                            o * block : (o + 1) * block
                        ]
                    continue
                turned = lax.dot_general(
                    select,
                    og[ks, rs],
                    (((1,), (1,)), ((), ())),
                    preferred_element_type=jnp.float32,
                ).astype(jnp.bfloat16)
                for h in range(2):
                    at = h * (rows // 2) + r * (tile // 2)
                    og_t[pl.ds(pl.multiple_of(at, tile // 2), tile // 2), ks] = turned[
                        h * (tile // 2) : (h + 1) * (tile // 2)
                    ]
            return 0

        lax.fori_loop(0, rows // tile, transpose, 0, unroll=rows <= 2 * tile)

    def multiply(j, size, first, last):
        def group(g, _):
            at = pl.ds(pl.multiple_of(g * size, size), size)
            part = jnp.dot(
                og_t[at, :], ins[j % SLOTS], preferred_element_type=jnp.float32
            )
            for o in range(size // block):
                at = g * (size // block) + o
                for q in range(share_of):
                    own = at // (dp // 2)
                    places = [
                        sum(
                            lax.rem(bit(me, b) + bit(at, b - 1), 2) * (dp >> (s + 1))
                            for s, b in enumerate(order)
                            if s
                        )
                        for order in orders
                    ]
                    place = chosen(q, own * core + (1 - own) * (1 - core), places)
                    acc[j, 1 - own, q, place] = part[o * block : (o + 1) * block, cols(q)]
            return 0

        lax.fori_loop(first // size, last // size, group, 0)

    def receive(s, j):
        half = dp >> (s + 1)
        held = (j // share_of, 0, j % share_of)
        exchange(s, j).wait_recv()
        if s < bits - 1:
            acc[(*held, pl.ds(0, half))] += recv[s][j]
            exchange(s + 1, j).start()
            return
        if j == 0:
            for copy in wms_copies:
                copy.wait()
        grad = acc[(*held, 0)] + recv[s][j, 0]
        moved, new_moment, new_second = finish(
            grad, wms[0, :, cols(j)], wms[1, :, cols(j)], wms[2, :, cols(j)]
        )
        moved_ref[:, cols(j)] = moved
        moment_ref[:, cols(j)] = new_moment
        second_ref[:, cols(j)] = new_second
        square = moved * moved
        tot[...] = square if j == 0 else tot[...] + square

    def sum_cores(j):
        swap(j).wait_recv()
        for q in range(share_of):
            acc[j, 0, q] += recv[0][j, q]
            exchange(1, j * share_of + q).start()

    def each(j, action):
        for q in range(share_of):
            action(j * share_of + q)

    for j in range(n):
        in_copy(j).wait()
        if j < SPLIT:
            multiply(j, GROUP // 2, 0, rows // 2)
            if j == 0:
                pl.semaphore_wait(barrier, bits + nt - 1)
            swap(j).start()
            if j:
                sum_cores(j - 1)
            multiply(j, GROUP // 2, rows // 2, rows)
        else:
            multiply(j, GROUP, 0, rows)
            swap(j).start()
            sum_cores(j - 1)
        if j >= AHEAD:
            each(j - AHEAD, lambda q: receive(1, q))
        if j == 0:
            for copy in wms_copies:
                copy.start()
        if j + SLOTS < n:
            in_copy(j + SLOTS).start()
    sum_cores(n - 1)
    for s in range(1, bits):
        for j in range(max(n - AHEAD, 0) * share_of if s == 1 else 0, parts):
            receive(s, j)

    def pair_of(value, axis):
        high = value.astype(jnp.bfloat16)
        rest = (value - high.astype(jnp.float32)).astype(jnp.bfloat16)
        return jnp.concatenate([high, rest], axis=axis)

    zsend[...] = lax.dot_general(
        jnp.ones((8, 256), jnp.bfloat16),
        pair_of(tot[...], 1),
        (((1,), (1,)), ((), ())),
        preferred_element_type=jnp.float32,
    )

    def share(d):
        return pltpu.make_async_remote_copy(
            src_ref=zsend,
            dst_ref=zrecv.at[d],
            send_sem=zs_sem.at[d],
            recv_sem=zr_sem.at[d],
            device_id=(me, peers[d]),
            device_id_type=MESH,
        )

    for d in range(nt - 1):
        share(d).start()
    for j in range(n):
        swap(j).wait_send()
    for s in range(1, bits):
        for j in range(parts):
            exchange(s, j).wait_send()
    for d in range(nt - 1):
        share(d).wait_send()
    total = zsend[...]
    for d in range(nt - 1):
        share(d).wait_recv()
        total = total + zrecv[d]
    row_total = lax.dot_general(
        pair_of(total, 0),
        jnp.full((16, 128), 0.125, jnp.bfloat16),
        (((0,), (0,)), ((), ())),
        preferred_element_type=jnp.float32,
    )
    out_scale[...] = lax.rsqrt(row_total / (width * nt) + 1e-06)


def write_kernel(moved, moment, second, scale, out_w, out_m, out_s, scaled, sem):
    copies = [
        pltpu.make_async_copy(src, dst, sem.at[i])
        for i, (src, dst) in enumerate(((scaled, out_w), (moment, out_m), (second, out_s)))
    ]
    copies[1].start()
    copies[2].start()
    for c in range(moved.shape[1] // 128):
        cs = slice(c * 128, (c + 1) * 128)
        scaled[:, cs] = moved[:, cs] * scale[...]
    copies[0].start()
    for copy in copies:
        copy.wait()


def on_device(dp, nt, out_grad, inputs, weights, moment, second):
    tokens, rows = out_grad.shape
    block, width = weights.shape
    parts = width // PART
    bits = dp.bit_length() - 1
    dma = pltpu.SemaphoreType.DMA
    scratch = [
        pltpu.VMEM((tokens, rows), jnp.bfloat16),
        pltpu.VMEM((rows, tokens), jnp.bfloat16),
        pltpu.VMEM((SLOTS, tokens, CHUNK), jnp.bfloat16),
        pltpu.VMEM((3, block, width), jnp.float32),
        pltpu.VMEM((width // CHUNK, 2, CHUNK // PART, dp // 2, block, PART), jnp.float32),
        pltpu.VMEM((block, 128), jnp.float32),
        pltpu.VMEM((8, block), jnp.float32),
        pltpu.VMEM((nt - 1, 8, block), jnp.float32),
    ]
    scratch += [
        pltpu.VMEM((width // CHUNK, CHUNK // PART, dp // 2, block, PART), jnp.float32)
    ]
    scratch += [
        pltpu.VMEM((parts, dp >> (s + 1), block, PART), jnp.float32) for s in range(1, bits)
    ]
    scratch += [
        dma((PIECES,)),
        dma((SLOTS,)),
        dma((3,)),
        dma((bits, parts)),
        dma((bits, parts)),
        dma((nt - 1,)),
        dma((nt - 1,)),
    ]
    held = sum(
        jnp.dtype(ref.dtype).itemsize * math.prod(ref.shape)
        for ref in scratch
        if getattr(ref, "memory_space", None) == pltpu.VMEM
    )
    shapes = [weights.shape] * 3 + [(block, 128)]
    results = pl.pallas_call(
        functools.partial(kernel, dp, nt),
        out_shape=[pltpu.VMEM(shape, jnp.float32) for shape in shapes],
        in_specs=[pl.BlockSpec(memory_space=pltpu.HBM)] * 5,
        out_specs=[pl.BlockSpec(memory_space=pltpu.VMEM)] * 4,
        scratch_shapes=scratch,
        compiler_params=pltpu.CompilerParams(
            collective_id=0, has_side_effects=True, vmem_limit_bytes=held + (3 << 20)
        ),
    )(
        *(
            pltpu.with_memory_space_constraint(x, pltpu.HBM)
            for x in (out_grad, inputs, weights, moment, second)
        )
    )
    return pl.pallas_call(
        write_kernel,
        out_shape=[pltpu.HBM(weights.shape, jnp.float32)] * 3,
        in_specs=[pl.BlockSpec(memory_space=pltpu.VMEM)] * 4,
        out_specs=[pl.BlockSpec(memory_space=pltpu.HBM)] * 3,
        scratch_shapes=[pltpu.VMEM(weights.shape, jnp.float32), dma((3,))],
        compiler_params=pltpu.CompilerParams(vmem_limit_bytes=2 << 20),
    )(*results)


def solution(mesh):
    held = P("dp", "tensor")
    return jax.shard_map(
        functools.partial(on_device, mesh.shape["dp"], mesh.shape["tensor"]),
        mesh=mesh,
        in_specs=(P("dp", None), held, held, held, held),
        out_specs=(held, held, held),
        check_vma=False,
    )
```
